32 devices in a mesh: seq: 8 (over z, y), tensor: 4 (over x, core).
Axes of the slice: x: 2, y: 2, z: 4, core: 2. Of those that a mesh axis runs over, the one named last changes fastest.
Arguments:
- inputs: bfloat16 [2, 1024, 4096], P(None, 'seq', 'tensor'), may hold values from -600 to 600
- norm_gain: float32 [4096], replicated, may hold values from 0.1 to 1.9
- w_query: bfloat16 [4096, 2048], P('seq', 'tensor'), may hold values from -0.09375 to 0.09375
- w_key: bfloat16 [4096, 2048], P('seq', 'tensor'), may hold values from -0.09375 to 0.09375
- w_value: bfloat16 [4096, 2048], P('seq', 'tensor'), may hold values from -0.09375 to 0.09375
- random_head_directions: bfloat16 [16, 256, 128], P('tensor'), may hold values from -6 to 6
Outputs:
- attended: bfloat16 [2, 1024, 2048], P(None, 'seq', 'tensor')
The draws below stay inside these ranges and needn't reach their ends.
All inputs are finite; a program needn't handle non-finite values.
Results may differ from the reference program's by a relative error of at most 0.012.
The reference program's roundings to bfloat16 on the way count: a program that leaves them out, or rounds other values in their place, can miss the bound.
Values may be sent and summed in bfloat16 or wider, within the bound.
A program may use at most 192 MiB of HBM per device.

```python
import math
import jax
import jax.numpy as jnp
from jax import lax

D = 4096
HEADS = 16
HEAD_SIZE = 128
M = 256
BATCH = 2
SEQ_DEV = 128
TOKEN_LENGTH = 1024
N_SEQ = 8


def draw_inputs(key, part):
    key_base, key_rows, key_cols = jax.random.split(key, 3)
    row_scale = jnp.exp(jax.random.uniform(key_rows, (BATCH, TOKEN_LENGTH, 1), jnp.float32) * math.log(10.0))
    col_scale = jnp.exp(jax.random.uniform(key_cols, (D,), jnp.float32) * math.log(10.0))
    base = jax.random.normal(key_base, (BATCH, TOKEN_LENGTH, D), jnp.float32)
    base = jnp.clip(base, -6.0, 6.0)
    return (base * row_scale * col_scale).astype(jnp.bfloat16)


def level_of(own_key, extent, shards, smallest, top_value):
    def one(axis_at, shards_of):
        heights = jax.random.uniform(jax.random.fold_in(jax.random.fold_in(own_key, 6), axis_at), (shards_of,), jnp.float32, smallest / len(shards), top_value / len(shards))
        return jnp.repeat(jnp.exp(heights), extent[axis_at] // shards_of).reshape((-1,) + (1,) * (len(extent) - axis_at - 1))

    level = one(*shards[0])
    for cut in shards[1:]:
        level = level * one(*cut)
    return level


def bell_draw(stream_key, shape, deviation, limit, cuts=(), kind=jnp.bfloat16):
    array = deviation * jax.random.normal(stream_key, shape, jnp.float32)
    if cuts:
        array = array * level_of(stream_key, shape, cuts, -0.22, 0.18)
    return jnp.clip(array, -limit, limit).astype(kind)


def setup_inputs(seed: int = 0) -> dict:
    splits = jax.random.split(jax.random.key(seed), 7)
    inputs = draw_inputs(jax.random.fold_in(splits[6], 71), 0)
    norm_gain = jnp.clip(1.0 + 0.18 * jax.random.normal(splits[1], (D,), jnp.float32), 0.1, 1.9)
    w_query = bell_draw(splits[2], (D, HEADS * HEAD_SIZE), D ** -0.5, 0.09375, ((0, 8), (1, 4)))
    w_key = bell_draw(splits[3], (D, HEADS * HEAD_SIZE), D ** -0.5, 0.09375, ((0, 8), (1, 4)))
    w_value = bell_draw(splits[4], (D, HEADS * HEAD_SIZE), D ** -0.5, 0.09375, ((0, 8), (1, 4)))
    random_head_directions = bell_draw(splits[5], (HEADS, M, HEAD_SIZE), 1.0, 6.0, ((0, 4),))
    return dict(inputs=inputs, norm_gain=norm_gain, w_query=w_query, w_key=w_key, w_value=w_value, random_head_directions=random_head_directions)


def rounded(values):
    return lax.optimization_barrier(values.astype(jnp.bfloat16)).astype(jnp.float32)

def feature_map(direction_product, random_head_directions):
    attention_logits = jnp.einsum('swcv,clv->swcl', direction_product, random_head_directions.astype(jnp.float32), precision=lax.Precision.HIGHEST) * HEAD_SIZE ** (-0.25)
    half_sq = 0.5 * lax.optimization_barrier(jnp.sum(direction_product * direction_product, axis=-1, keepdims=True)) * HEAD_SIZE ** (-0.5)
    return rounded(jnp.exp(attention_logits - half_sq) * M ** (-0.5))

def reference(inputs, norm_gain, w_query, w_key, w_value, random_head_directions):
    wide_in = inputs.astype(jnp.float32)
    inv_rms = lax.rsqrt(lax.optimization_barrier(jnp.mean(wide_in * wide_in, axis=-1, keepdims=True)) + 1e-05)
    normed = (wide_in * inv_rms * norm_gain).astype(jnp.bfloat16).reshape(BATCH * TOKEN_LENGTH, D)

    def project(weight):
        result = rounded(jnp.dot(normed, weight, preferred_element_type=jnp.float32))
        return jnp.moveaxis(result.reshape(BATCH, N_SEQ, SEQ_DEV, HEADS, HEAD_SIZE), 1, 0)
    query = project(w_query)
    keys = project(w_key)
    values = project(w_value)
    lower_triangle_mask = jnp.tril(jnp.ones((SEQ_DEV, SEQ_DEV), jnp.bool_))
    highest = lax.Precision.HIGHEST

    def block_step(carried, blocks):
        kv_state, key_sum = carried
        query_blk, key_blk, value_blk = blocks
        phi_query = feature_map(query_blk, random_head_directions)
        phi_key = feature_map(key_blk, random_head_directions)
        scores = jnp.where(lower_triangle_mask, jnp.einsum('bihm,bjhm->bhij', phi_query, phi_key, precision=highest), jnp.float32(0.0))
        denom_local = lax.optimization_barrier(jnp.sum(scores, axis=-1))
        numer_local = jnp.einsum('bhij,bjhd->bihd', rounded(scores), value_blk, precision=highest)
        numer_carried = jnp.einsum('bihm,bhmd->bihd', phi_query, rounded(kv_state), precision=highest)
        denom_carried = jnp.einsum('bihm,bhm->bih', phi_query, key_sum, precision=highest)
        numer = numer_local + numer_carried
        denom = jnp.transpose(denom_local, (0, 2, 1)) + denom_carried
        output = (numer / denom[..., None]).astype(jnp.bfloat16)
        kv_state = kv_state + jnp.einsum('bjhm,bjhd->bhmd', phi_key, value_blk, precision=highest)
        key_sum = key_sum + lax.optimization_barrier(jnp.sum(phi_key, axis=1))
        return ((kv_state, key_sum), output)
    initial = (jnp.zeros((BATCH, HEADS, M, HEAD_SIZE), jnp.float32), jnp.zeros((BATCH, HEADS, M), jnp.float32))
    finals, outputs = lax.scan(block_step, initial, (query, keys, values))
    return jnp.moveaxis(outputs, 0, 1).reshape(BATCH, TOKEN_LENGTH, HEADS * HEAD_SIZE)
```

```python
import functools
import jax
import jax.numpy as jnp
from jax import lax
from jax.experimental import pallas as pl
from jax.experimental.pallas import tpu as pltpu
from jax.sharding import PartitionSpec as P

MESH = pl.DeviceIdType.MESH
F32 = jnp.float32
BF16 = jnp.bfloat16


def head_kernel(
    nz, x_ref, gain_ref, wq_ref, wk_ref, wv_ref, dir_ref, out_ref,
    norm, weight, packed, other, squares, qkv, acc, kv_ref, ksum_ref, made, landed,
    ss_send, ss_recv, b_send, b_recv, z_send, z_recv, x_send, x_recv, c_send, c_recv,
    w_send, w_recv, f_send, f_recv, o_send, o_recv,
):
    s, t = lax.axis_index("seq"), lax.axis_index("tensor")
    z, y = s // 2, s % 2
    ns = 2 * nz
    x, c = t // 2, t % 2
    ty, tx, tc = s + 1 - 2 * y, t + 2 - 4 * x, t + 1 - 2 * c
    tx_c = tx + 1 - 2 * c
    rows, width = x_ref.shape[1], x_ref.shape[2]
    depth = wq_ref.shape[0]
    hd = wq_ref.shape[1] // nz
    full = 4 * width

    def copy(src, dst, send, recv, ds, dt):
        return pltpu.make_async_remote_copy(
            src_ref=src, dst_ref=dst, send_sem=send, recv_sem=recv,
            device_id=(ds, dt), device_id_type=MESH,
        )

    def block(ti, sp):
        return norm.at[ti, pl.ds(pl.multiple_of(sp * rows, rows), rows), :]

    def wrows(sp):
        return weight.at[pl.ds(pl.multiple_of(sp * depth, depth), depth), :]

    barrier = pltpu.get_barrier_semaphore()
    for d in range(1, ns):
        pl.semaphore_signal(barrier, inc=1, device_id=((s + d) % ns, t), device_id_type=MESH)
    for d in range(1, 4):
        pl.semaphore_signal(barrier, inc=1, device_id=(s, (t + d) % 4), device_id_type=MESH)

    for b in range(2):
        wide = x_ref[b].astype(F32)
        part = jnp.sum(wide * wide, axis=-1, keepdims=True)
        lanes = jnp.broadcast_to(part, (rows, 128)).T
        squares[t, :, pl.ds(b * rows, rows)] = lanes[0:8]
    for h in range(nz):
        for j, w_ref in enumerate((wq_ref, wk_ref, wv_ref)):
            packed[h, :, j * hd:(j + 1) * hd] = w_ref[:, h * hd:(h + 1) * hd]
    pl.semaphore_wait(barrier, ns - 1 + 3)

    def ss_copy(d):
        return copy(squares.at[t], squares.at[t], ss_send.at[d], ss_recv.at[d], s, (t + d) % 4)

    for d in range(1, 4):
        ss_copy(d).start()

    def w_copy(d):
        to = (z + d) % nz
        return copy(packed.at[to], wrows(s), w_send.at[d], w_recv.at[d], 2 * to + y, t)

    def f_copy(zs):
        return copy(wrows(2 * zs + y), wrows(2 * zs + y), f_send.at[zs], f_recv.at[zs], ty, t)

    weight[pl.ds(pl.multiple_of(s * depth, depth), depth), :] = packed[z]
    f_copy(z).start()
    for d in range(1, nz):
        w_copy(d).start()

    for d in range(1, 4):
        src = (t + 4 - d) % 4
        copy(squares.at[t], squares.at[src], ss_send.at[d], ss_recv.at[d], s, t).wait_recv()
    total = squares[0] + squares[1] + squares[2] + squares[3]
    gain = gain_ref[:, pl.ds(pl.multiple_of(t * width, width), width)]

    def normed(b):
        sums = total[0:1, b * rows:(b + 1) * rows]
        column = jnp.broadcast_to(sums, (128, rows)).T
        inv = lax.rsqrt(column[:, 0:1] * (1.0 / full) + 1e-05)
        return (x_ref[b].astype(F32) * inv * gain).astype(BF16)

    for b in range(2):
        @pl.when(y == b)
        def _():
            norm[t, pl.ds(pl.multiple_of(s * rows, rows), rows), :] = normed(b)
            other[...] = normed(1 - b)

    b_copy = copy(other, block(t, s), b_send, b_recv, ty, t)
    b_copy.start()

    def right(sp):
        return copy(block(t, sp), block(t, sp), z_send.at[0, sp], z_recv.at[sp], s + 2, t)

    def left(sp):
        return copy(block(t, sp), block(t, sp), z_send.at[1, sp], z_recv.at[sp], s - 2, t)

    def x_copy(sp):
        return copy(block(t, sp), block(t, sp), x_send.at[sp], x_recv.at[sp], s, tx)

    def c_copy(kind, ti, sp):
        return copy(block(ti, sp), block(ti, sp), c_send.at[kind, sp], c_recv.at[kind, sp], s, tc)

    def spread(sp):
        x_copy(sp).start()
        c_copy(0, t, sp).start()

    def relay(sp):
        copy(block(t, sp), block(tx, sp), x_send.at[sp], x_recv.at[sp], s, tx).wait_recv()
        c_copy(1, tx, sp).start()

    def go(sp):
        @pl.when(z + 1 < nz)
        def _():
            right(sp).start()

        @pl.when(z > 0)
        def _():
            left(sp).start()

    go(s)
    spread(s)
    copy(other, block(t, ty), b_send, b_recv, ty, t).wait_recv()
    go(ty)
    spread(ty)
    relay(s)
    relay(ty)

    def arrivals(k, act):
        for h in range(2):
            from_left = 2 * (z - 1 - k) + (y + h) % 2
            from_right = 2 * (z + 1 + k) + (y + h) % 2

            @pl.when(z - 1 - k >= 0)
            def _():
                act(from_left, 0)

            @pl.when(z + 1 + k < nz)
            def _():
                act(from_right, 1)

    def take(sp, side):
        copy(block(t, sp), block(t, sp), z_send.at[0, sp], z_recv.at[sp], s, t).wait_recv()
        if side == 0:
            @pl.when(z + 1 < nz)
            def _():
                right(sp).start()
        else:
            @pl.when(z > 0)
            def _():
                left(sp).start()
        spread(sp)

    for k in range(nz - 1):
        arrivals(k, take)
        arrivals(k, lambda sp, side: relay(sp))

    for d in range(1, nz):
        zs = (z + nz - d) % nz
        copy(packed.at[z], wrows(2 * zs + y), w_send.at[d], w_recv.at[d], s, t).wait_recv()
        f_copy(zs).start()

    for sp in range(ns):
        copy(block(t, sp), block(tc, sp), c_send.at[0, sp], c_recv.at[0, sp], s, tc).wait_recv()
        copy(block(tx, sp), block(tx_c, sp), c_send.at[1, sp], c_recv.at[1, sp], s, tc).wait_recv()
    for zs in range(nz):
        theirs = wrows(2 * zs + 1 - y)
        copy(theirs, theirs, f_send.at[zs], f_recv.at[zs], ty, t).wait_recv()

    chunk = 2 * rows

    def project(i, carry):
        at = pl.ds(pl.multiple_of(i * chunk, chunk), chunk)
        result = jnp.dot(norm[0, at, :], weight[0:width, :], preferred_element_type=F32)
        for ti in range(1, 4):
            result += jnp.dot(
                norm[ti, at, :], weight[ti * width:(ti + 1) * width, :], preferred_element_type=F32
            )
        qkv[at, :] = result.astype(BF16)
        return carry

    lax.fori_loop(0, nz, project, 0)

    directions = dir_ref[z]
    count = directions.shape[0]
    nt = (((1,), (1,)), ((), ()))
    tn = (((0,), (0,)), ((), ()))

    def features(u):
        logits = lax.dot_general(u, directions, nt, preferred_element_type=F32) * hd ** (-0.25)
        wide = u.astype(F32)
        half_sq = 0.5 * jnp.sum(wide * wide, axis=-1, keepdims=True) * hd ** (-0.5)
        return (jnp.exp(logits - half_sq) * count ** (-0.5)).astype(BF16)

    kv_ref[...] = jnp.zeros_like(kv_ref)
    ksum_ref[...] = jnp.zeros_like(ksum_ref)
    row_id = lax.broadcasted_iota(jnp.int32, (rows, rows), 0)
    col_id = lax.broadcasted_iota(jnp.int32, (rows, rows), 1)

    def o_copy(i):
        return copy(made.at[i], landed.at[s], o_send.at[i], o_recv.at[s], i, t)

    def attend(i, carry):
        at = pl.ds(pl.multiple_of(i * rows, rows), rows)
        phi_query = features(qkv[at, 0:hd])
        phi_key = features(qkv[at, hd:2 * hd])
        value = qkv[at, 2 * hd:3 * hd]
        scores = lax.dot_general(phi_query, phi_key, nt, preferred_element_type=F32)
        scores = jnp.where(col_id <= row_id, scores, 0.0)
        ksum = ksum_ref[0:1, :]
        denom = jnp.sum(scores, axis=-1, keepdims=True) + jnp.sum(
            phi_query.astype(F32) * ksum, axis=-1, keepdims=True
        )
        numer = jnp.dot(scores.astype(BF16), value, preferred_element_type=F32) + jnp.dot(
            phi_query, kv_ref[...].astype(BF16), preferred_element_type=F32
        )
        made[i] = (numer / denom).astype(BF16)

        @pl.when(i != s)
        def _():
            o_copy(i).start()

        kv_ref[...] += lax.dot_general(phi_key, value, tn, preferred_element_type=F32)
        ksum_ref[0:1, :] = ksum + jnp.sum(phi_key.astype(F32), axis=0, keepdims=True)
        return carry

    lax.fori_loop(0, ns, attend, 0)

    for sp in range(ns):
        @pl.when(sp != s)
        def _():
            copy(made.at[sp], landed.at[sp], o_send.at[sp], o_recv.at[sp], sp, t).wait_recv()

        @pl.when(sp == s)
        def _():
            landed[sp] = made[sp]

        out_ref[sp % 2, :, (sp // 2) * hd:(sp // 2 + 1) * hd] = landed[sp]

    for d in range(1, 4):
        ss_copy(d).wait_send()
    for d in range(1, nz):
        w_copy(d).wait_send()
    for zs in range(nz):
        f_copy(zs).wait_send()
    b_copy.wait_send()
    for sp in range(ns):
        x_copy(sp).wait_send()
        c_copy(0, t, sp).wait_send()
        c_copy(1, tx, sp).wait_send()

        @pl.when((sp // 2 <= z) & (z + 1 < nz))
        def _():
            right(sp).wait_send()

        @pl.when((sp // 2 >= z) & (z > 0))
        def _():
            left(sp).wait_send()

        @pl.when(sp != s)
        def _():
            o_copy(sp).wait_send()


def by_head(inputs, norm_gain, w_query, w_key, w_value, random_head_directions):
    ns = lax.axis_size("seq")
    nz = ns // 2
    batch, rows, width = inputs.shape
    depth, columns = w_query.shape
    hd = columns // nz
    count = random_head_directions.shape[1]
    dma = pltpu.SemaphoreType.DMA
    return pl.pallas_call(
        functools.partial(head_kernel, nz),
        out_shape=jax.ShapeDtypeStruct((batch, rows, columns), BF16),
        in_specs=[pl.BlockSpec(memory_space=pltpu.VMEM)] * 6,
        out_specs=pl.BlockSpec(memory_space=pltpu.VMEM),
        scratch_shapes=[
            pltpu.VMEM((4, ns * rows, width), BF16),
            pltpu.VMEM((ns * depth, 3 * hd), BF16),
            pltpu.VMEM((nz, depth, 3 * hd), BF16),
            pltpu.VMEM((rows, width), BF16),
            pltpu.VMEM((4, 8, 2 * rows), F32),
            pltpu.VMEM((ns * rows, 3 * hd), BF16),
            pltpu.VMEM((8, 128), F32),
            pltpu.VMEM((count, hd), F32),
            pltpu.VMEM((8, count), F32),
            pltpu.VMEM((ns, rows, hd), BF16),
            pltpu.VMEM((ns, rows, hd), BF16),
            dma((4,)), dma((4,)), dma, dma, dma((2, ns)), dma((ns,)), dma((ns,)), dma((ns,)),
            dma((2, ns)), dma((2, ns)), dma((nz,)), dma((nz,)), dma((nz,)), dma((nz,)),
            dma((ns,)), dma((ns,)),
        ],
        compiler_params=pltpu.CompilerParams(
            collective_id=0, has_side_effects=True, vmem_limit_bytes=48 * 1024 * 1024
        ),
    )(inputs, norm_gain.reshape(1, -1), w_query, w_key, w_value, random_head_directions)


def carried_in(value, axis, join, neutral):
    count, mine = (lax.axis_size(axis), lax.axis_index(axis))
    pieces = jax.tree.map(lambda part: lax.all_gather(part, axis), value)
    total = jax.tree.map(
        lambda part, zero: jnp.full_like(part, 0) + jnp.asarray(zero, part.dtype), value, neutral
    )

    def hop(position, total):
        longer = join(total, jax.tree.map(lambda part: part[position], pieces))
        return jax.tree.map(lambda new, old: jnp.where(position < mine, new, old), longer, total)

    return lax.fori_loop(0, count - 1, hop, total)


def feature_map(direction_product, random_head_directions):
    head_dim = direction_product.shape[-1]
    feature_count = random_head_directions.shape[1]
    attention_logits = jnp.einsum(
        "swcv,clv->swcl",
        direction_product,
        random_head_directions,
        preferred_element_type=jnp.float32,
    ) * head_dim ** (-0.25)
    squared = direction_product.astype(jnp.float32)
    half_sq = 0.5 * jnp.sum(squared * squared, axis=-1, keepdims=True) * head_dim ** (-0.5)
    return (jnp.exp(attention_logits - half_sq) * feature_count ** (-0.5)).astype(jnp.bfloat16)


def add_pair(earlier, later):
    return (earlier[0] + later[0], earlier[1] + later[1])


def on_device(inputs, norm_gain, w_query, w_key, w_value, random_head_directions):
    gathered = lax.all_gather(inputs, "tensor", axis=2, tiled=True)
    batch_size, row_count, full_width = gathered.shape
    wide_in = gathered.astype(jnp.float32)
    inv_rms = lax.rsqrt(jnp.mean(wide_in * wide_in, axis=-1, keepdims=True) + 1e-05)
    normed = (
        (wide_in * inv_rms * norm_gain)
        .astype(jnp.bfloat16)
        .reshape(batch_size * row_count, full_width)
    )

    def add_rows(portion):
        return jnp.dot(normed, portion, preferred_element_type=jnp.float32)

    query_acc = add_rows(lax.all_gather(w_query, "seq", axis=0, tiled=True))
    key_acc = add_rows(lax.all_gather(w_key, "seq", axis=0, tiled=True))
    value_total = add_rows(lax.all_gather(w_value, "seq", axis=0, tiled=True))
    head_count, feature_count, head_dim = random_head_directions.shape

    def split_heads(accum):
        return accum.astype(jnp.bfloat16).reshape(batch_size, row_count, head_count, head_dim)

    query = split_heads(query_acc)
    keys = split_heads(key_acc)
    values = split_heads(value_total)
    phi_query = feature_map(query, random_head_directions)
    phi_key = feature_map(keys, random_head_directions)
    kv_state = jnp.einsum("bjhm,bjhd->bhmd", phi_key, values, preferred_element_type=jnp.float32)
    key_total = jnp.sum(phi_key.astype(jnp.float32), axis=1)
    zero_pair = (jnp.zeros_like(kv_state), jnp.zeros_like(key_total))
    kv_prefix, key_prefix = carried_in((kv_state, key_total), "seq", add_pair, zero_pair)
    lower_triangle_mask = jnp.tril(jnp.ones((row_count, row_count), jnp.bool_))
    scores = jnp.einsum("bihm,bjhm->bhij", phi_query, phi_key, preferred_element_type=jnp.float32)
    scores = jnp.where(lower_triangle_mask, scores, jnp.float32(0.0))
    denom_local = jnp.transpose(jnp.sum(scores, axis=-1), (0, 2, 1))
    numer_local = jnp.einsum(
        "bhij,bjhd->bihd", scores.astype(jnp.bfloat16), values, preferred_element_type=jnp.float32
    )
    numer_local, denom_local = (numer_local, denom_local)
    numer_carried = jnp.einsum(
        "bihm,bhmd->bihd",
        phi_query,
        kv_prefix.astype(jnp.bfloat16),
        preferred_element_type=jnp.float32,
    )
    denom_carried = jnp.einsum(
        "bihm,bhm->bih", phi_query.astype(jnp.float32), key_prefix, precision=lax.Precision.HIGHEST
    )
    numer = numer_local + numer_carried
    denom = denom_local + denom_carried
    output = (numer / denom[..., None]).astype(jnp.bfloat16)
    return output.reshape(batch_size, row_count, head_count * head_dim)


def solution(mesh):
    in_specs = (
        P(None, "seq", "tensor"),
        P(),
        P("seq", "tensor"),
        P("seq", "tensor"),
        P("seq", "tensor"),
        P("tensor", None, None),
    )
    out_specs = P(None, "seq", "tensor")
    fits = mesh.shape["seq"] == 8 and mesh.shape["tensor"] == 4
    return jax.shard_map(
        by_head if fits else on_device, mesh=mesh, in_specs=in_specs, out_specs=out_specs, check_vma=False
    )
```

```python
import functools
import jax
import jax.numpy as jnp
from jax import lax
from jax.experimental import pallas as pl
from jax.experimental.pallas import tpu as pltpu
from jax.sharding import PartitionSpec as P

MESH = pl.DeviceIdType.MESH
F32 = jnp.float32
BF16 = jnp.bfloat16


def head_kernel(
    nz, x_ref, gain_ref, wq_ref, wk_ref, wv_ref, dir_ref, out_ref,
    norm, weight, packed, other, squares, qkv, kv_ref, ksum_ref, made, landed,
    ss_send, ss_recv, b_send, b_recv, z_send, z_recv, x_send, x_recv, c_send, c_recv,
    w_send, w_recv, f_send, f_recv, o_send, o_recv,
):
    s, t = lax.axis_index("seq"), lax.axis_index("tensor")
    z, y = s // 2, s % 2
    ns = 2 * nz
    x, c = t // 2, t % 2
    ty, tx, tc = s + 1 - 2 * y, t + 2 - 4 * x, t + 1 - 2 * c
    tx_c = tx + 1 - 2 * c
    rows, width = x_ref.shape[1], x_ref.shape[2]
    depth = wq_ref.shape[0]
    hd = wq_ref.shape[1] // nz
    full = 4 * width

    def copy(src, dst, send, recv, ds, dt):
        return pltpu.make_async_remote_copy(
            src_ref=src, dst_ref=dst, send_sem=send, recv_sem=recv,
            device_id=(ds, dt), device_id_type=MESH,
        )

    def block(ti, sp):
        return norm.at[ti, pl.ds(pl.multiple_of(sp * rows, rows), rows), :]

    def wrows(sp):
        return weight.at[pl.ds(pl.multiple_of(sp * depth, depth), depth), :]

    barrier = pltpu.get_barrier_semaphore()
    for d in range(1, ns):
        pl.semaphore_signal(barrier, inc=1, device_id=((s + d) % ns, t), device_id_type=MESH)
    for d in range(1, 4):
        pl.semaphore_signal(barrier, inc=1, device_id=(s, (t + d) % 4), device_id_type=MESH)

    for b in range(2):
        wide = x_ref[b].astype(F32)
        part = jnp.sum(wide * wide, axis=-1, keepdims=True)
        lanes = jnp.broadcast_to(part, (rows, 128)).T
        squares[t, :, pl.ds(b * rows, rows)] = lanes[0:8]
    for h in range(nz):
        for j, w_ref in enumerate((wq_ref, wk_ref, wv_ref)):
            packed[h, :, j * hd:(j + 1) * hd] = w_ref[:, h * hd:(h + 1) * hd]
    pl.semaphore_wait(barrier, ns - 1 + 3)

    def ss_copy(d):
        return copy(squares.at[t], squares.at[t], ss_send.at[d], ss_recv.at[d], s, (t + d) % 4)

    for d in range(1, 4):
        ss_copy(d).start()

    def w_copy(to):
        return copy(packed.at[to], wrows(s), w_send.at[to], w_recv.at[z], 2 * to + y, t)

    def each_side(distance, act):
        @pl.when(z - distance >= 0)
        def _():
            act(z - distance)

        @pl.when(z + distance < nz)
        def _():
            act(z + distance)

    def f_copy(zs):
        return copy(wrows(2 * zs + y), wrows(2 * zs + y), f_send.at[zs], f_recv.at[zs], ty, t)

    weight[pl.ds(pl.multiple_of(s * depth, depth), depth), :] = packed[z]
    f_copy(z).start()
    def w_out(distance):
        each_side(distance, lambda to: w_copy(to).start())

    def w_take(distance):
        def act(zs):
            rows_in = wrows(2 * zs + y)
            copy(rows_in, rows_in, w_send.at[zs], w_recv.at[zs], s, t).wait_recv()
            f_copy(zs).start()

        each_side(distance, act)

    for d in range(1, nz):
        w_out(d)

    for d in range(1, 4):
        src = (t + 4 - d) % 4
        copy(squares.at[t], squares.at[src], ss_send.at[d], ss_recv.at[d], s, t).wait_recv()
    total = squares[0] + squares[1] + squares[2] + squares[3]
    gain = gain_ref[:, pl.ds(pl.multiple_of(t * width, width), width)]

    def normed(b):
        sums = total[0:1, b * rows:(b + 1) * rows]
        column = jnp.broadcast_to(sums, (128, rows)).T
        inv = lax.rsqrt(column[:, 0:1] * (1.0 / full) + 1e-05)
        return (x_ref[b].astype(F32) * inv * gain).astype(BF16)

    for b in range(2):
        @pl.when(y == b)
        def _():
            norm[t, pl.ds(pl.multiple_of(s * rows, rows), rows), :] = normed(b)
            other[...] = normed(1 - b)

    b_copy = copy(other, block(t, s), b_send, b_recv, ty, t)
    b_copy.start()

    def right(sp):
        return copy(block(t, sp), block(t, sp), z_send.at[0, sp], z_recv.at[sp], s + 2, t)

    def left(sp):
        return copy(block(t, sp), block(t, sp), z_send.at[1, sp], z_recv.at[sp], s - 2, t)

    def x_copy(sp):
        return copy(block(t, sp), block(t, sp), x_send.at[sp], x_recv.at[sp], s, tx)

    def c_copy(kind, ti, sp):
        return copy(block(ti, sp), block(ti, sp), c_send.at[kind, sp], c_recv.at[kind, sp], s, tc)

    def spread(sp):
        x_copy(sp).start()
        c_copy(0, t, sp).start()

    def relay(sp):
        copy(block(t, sp), block(tx, sp), x_send.at[sp], x_recv.at[sp], s, tx).wait_recv()
        c_copy(1, tx, sp).start()

    def go(sp):
        @pl.when(z + 1 < nz)
        def _():
            right(sp).start()

        @pl.when(z > 0)
        def _():
            left(sp).start()

    go(s)
    spread(s)
    copy(other, block(t, ty), b_send, b_recv, ty, t).wait_recv()
    go(ty)
    spread(ty)
    relay(s)
    relay(ty)

    def arrivals(k, act):
        for h in range(2):
            from_left = 2 * (z - 1 - k) + (y + h) % 2
            from_right = 2 * (z + 1 + k) + (y + h) % 2

            @pl.when(z - 1 - k >= 0)
            def _():
                act(from_left, 0)

            @pl.when(z + 1 + k < nz)
            def _():
                act(from_right, 1)

    def take(sp, side):
        copy(block(t, sp), block(t, sp), z_send.at[0, sp], z_recv.at[sp], s, t).wait_recv()
        if side == 0:
            @pl.when(z + 1 < nz)
            def _():
                right(sp).start()
        else:
            @pl.when(z > 0)
            def _():
                left(sp).start()
        spread(sp)

    for k in range(nz - 1):
        arrivals(k, take)
        arrivals(k, lambda sp, side: relay(sp))
        w_take(k + 1)

    for sp in range(ns):
        copy(block(t, sp), block(tc, sp), c_send.at[0, sp], c_recv.at[0, sp], s, tc).wait_recv()
        copy(block(tx, sp), block(tx_c, sp), c_send.at[1, sp], c_recv.at[1, sp], s, tc).wait_recv()
    for zs in range(nz):
        theirs = wrows(2 * zs + 1 - y)
        copy(theirs, theirs, f_send.at[zs], f_recv.at[zs], ty, t).wait_recv()

    chunk = 2 * rows

    def project(i, carry):
        at = pl.ds(pl.multiple_of(i * chunk, chunk), chunk)
        result = jnp.dot(norm[0, at, :], weight[0:width, :], preferred_element_type=F32)
        for ti in range(1, 4):
            result += jnp.dot(
                norm[ti, at, :], weight[ti * width:(ti + 1) * width, :], preferred_element_type=F32
            )
        qkv[at, :] = result.astype(BF16)
        return carry

    lax.fori_loop(0, nz, project, 0)

    directions = dir_ref[z]
    count = directions.shape[0]
    nt = (((1,), (1,)), ((), ()))
    tn = (((0,), (0,)), ((), ()))

    def features(u):
        logits = lax.dot_general(u, directions, nt, preferred_element_type=F32) * hd ** (-0.25)
        wide = u.astype(F32)
        half_sq = 0.5 * jnp.sum(wide * wide, axis=-1, keepdims=True) * hd ** (-0.5)
        return (jnp.exp(logits - half_sq) * count ** (-0.5)).astype(BF16)

    kv_ref[...] = jnp.zeros_like(kv_ref)
    ksum_ref[...] = jnp.zeros_like(ksum_ref)
    row_id = lax.broadcasted_iota(jnp.int32, (rows, rows), 0)
    col_id = lax.broadcasted_iota(jnp.int32, (rows, rows), 1)

    def o_copy(i):
        return copy(made.at[i], landed.at[s], o_send.at[i], o_recv.at[s], i, t)

    def attend(i, carry):
        at = pl.ds(pl.multiple_of(i * rows, rows), rows)
        phi_query = features(qkv[at, 0:hd])
        phi_key = features(qkv[at, hd:2 * hd])
        value = qkv[at, 2 * hd:3 * hd]
        scores = lax.dot_general(phi_query, phi_key, nt, preferred_element_type=F32)
        scores = jnp.where(col_id <= row_id, scores, 0.0)
        ksum = ksum_ref[0:1, :]
        denom = jnp.sum(scores, axis=-1, keepdims=True) + jnp.sum(
            phi_query.astype(F32) * ksum, axis=-1, keepdims=True
        )
        numer = jnp.dot(scores.astype(BF16), value, preferred_element_type=F32) + jnp.dot(
            phi_query, kv_ref[...].astype(BF16), preferred_element_type=F32
        )
        made[i] = (numer / denom).astype(BF16)

        @pl.when(i != s)
        def _():
            o_copy(i).start()

        kv_ref[...] += lax.dot_general(phi_key, value, tn, preferred_element_type=F32)
        ksum_ref[0:1, :] = ksum + jnp.sum(phi_key.astype(F32), axis=0, keepdims=True)
        return carry

    lax.fori_loop(0, ns, attend, 0)

    for sp in range(ns):
        @pl.when(sp != s)
        def _():
            copy(made.at[sp], landed.at[sp], o_send.at[sp], o_recv.at[sp], sp, t).wait_recv()

        @pl.when(sp == s)
        def _():
            landed[sp] = made[sp]

        out_ref[sp % 2, :, (sp // 2) * hd:(sp // 2 + 1) * hd] = landed[sp]

    for d in range(1, 4):
        ss_copy(d).wait_send()
    for d in range(1, nz):
        each_side(d, lambda to: w_copy(to).wait_send())
    for zs in range(nz):
        f_copy(zs).wait_send()
    b_copy.wait_send()
    for sp in range(ns):
        x_copy(sp).wait_send()
        c_copy(0, t, sp).wait_send()
        c_copy(1, tx, sp).wait_send()

        @pl.when((sp // 2 <= z) & (z + 1 < nz))
        def _():
            right(sp).wait_send()

        @pl.when((sp // 2 >= z) & (z > 0))
        def _():
            left(sp).wait_send()

        @pl.when(sp != s)
        def _():
            o_copy(sp).wait_send()


def by_head(inputs, norm_gain, w_query, w_key, w_value, random_head_directions):
    ns = lax.axis_size("seq")
    nz = ns // 2
    batch, rows, width = inputs.shape
    depth, columns = w_query.shape
    hd = columns // nz
    count = random_head_directions.shape[1]
    dma = pltpu.SemaphoreType.DMA
    return pl.pallas_call(
        functools.partial(head_kernel, nz),
        out_shape=jax.ShapeDtypeStruct((batch, rows, columns), BF16),
        in_specs=[pl.BlockSpec(memory_space=pltpu.VMEM)] * 6,
        out_specs=pl.BlockSpec(memory_space=pltpu.VMEM),
        scratch_shapes=[
            pltpu.VMEM((4, ns * rows, width), BF16),
            pltpu.VMEM((ns * depth, 3 * hd), BF16),
            pltpu.VMEM((nz, depth, 3 * hd), BF16),
            pltpu.VMEM((rows, width), BF16),
            pltpu.VMEM((4, 8, 2 * rows), F32),
            pltpu.VMEM((ns * rows, 3 * hd), BF16),
            pltpu.VMEM((count, hd), F32),
            pltpu.VMEM((8, count), F32),
            pltpu.VMEM((ns, rows, hd), BF16),
            pltpu.VMEM((ns, rows, hd), BF16),
            dma((4,)), dma((4,)), dma, dma, dma((2, ns)), dma((ns,)), dma((ns,)), dma((ns,)),
            dma((2, ns)), dma((2, ns)), dma((nz,)), dma((nz,)), dma((nz,)), dma((nz,)),
            dma((ns,)), dma((ns,)),
        ],
        compiler_params=pltpu.CompilerParams(
            collective_id=0, has_side_effects=True, vmem_limit_bytes=48 * 1024 * 1024
        ),
    )(inputs, norm_gain.reshape(1, -1), w_query, w_key, w_value, random_head_directions)


def carried_in(value, axis, join, neutral):
    count, mine = (lax.axis_size(axis), lax.axis_index(axis))
    pieces = jax.tree.map(lambda part: lax.all_gather(part, axis), value)
    total = jax.tree.map(
        lambda part, zero: jnp.full_like(part, 0) + jnp.asarray(zero, part.dtype), value, neutral
    )

    def hop(position, total):
        longer = join(total, jax.tree.map(lambda part: part[position], pieces))
        return jax.tree.map(lambda new, old: jnp.where(position < mine, new, old), longer, total)

    return lax.fori_loop(0, count - 1, hop, total)


def feature_map(direction_product, random_head_directions):
    head_dim = direction_product.shape[-1]
    feature_count = random_head_directions.shape[1]
    attention_logits = jnp.einsum(
        "swcv,clv->swcl",
        direction_product,
        random_head_directions,
        preferred_element_type=jnp.float32,
    ) * head_dim ** (-0.25)
    squared = direction_product.astype(jnp.float32)
    half_sq = 0.5 * jnp.sum(squared * squared, axis=-1, keepdims=True) * head_dim ** (-0.5)
    return (jnp.exp(attention_logits - half_sq) * feature_count ** (-0.5)).astype(jnp.bfloat16)


def add_pair(earlier, later):
    return (earlier[0] + later[0], earlier[1] + later[1])


def on_device(inputs, norm_gain, w_query, w_key, w_value, random_head_directions):
    gathered = lax.all_gather(inputs, "tensor", axis=2, tiled=True)
    batch_size, row_count, full_width = gathered.shape
    wide_in = gathered.astype(jnp.float32)
    inv_rms = lax.rsqrt(jnp.mean(wide_in * wide_in, axis=-1, keepdims=True) + 1e-05)
    normed = (
        (wide_in * inv_rms * norm_gain)
        .astype(jnp.bfloat16)
        .reshape(batch_size * row_count, full_width)
    )

    def add_rows(portion):
        return jnp.dot(normed, portion, preferred_element_type=jnp.float32)

    query_acc = add_rows(lax.all_gather(w_query, "seq", axis=0, tiled=True))
    key_acc = add_rows(lax.all_gather(w_key, "seq", axis=0, tiled=True))
    value_total = add_rows(lax.all_gather(w_value, "seq", axis=0, tiled=True))
    head_count, feature_count, head_dim = random_head_directions.shape

    def split_heads(accum):
        return accum.astype(jnp.bfloat16).reshape(batch_size, row_count, head_count, head_dim)

    query = split_heads(query_acc)
    keys = split_heads(key_acc)
    values = split_heads(value_total)
    phi_query = feature_map(query, random_head_directions)
    phi_key = feature_map(keys, random_head_directions)
    kv_state = jnp.einsum("bjhm,bjhd->bhmd", phi_key, values, preferred_element_type=jnp.float32)
    key_total = jnp.sum(phi_key.astype(jnp.float32), axis=1)
    zero_pair = (jnp.zeros_like(kv_state), jnp.zeros_like(key_total))
    kv_prefix, key_prefix = carried_in((kv_state, key_total), "seq", add_pair, zero_pair)
    lower_triangle_mask = jnp.tril(jnp.ones((row_count, row_count), jnp.bool_))
    scores = jnp.einsum("bihm,bjhm->bhij", phi_query, phi_key, preferred_element_type=jnp.float32)
    scores = jnp.where(lower_triangle_mask, scores, jnp.float32(0.0))
    denom_local = jnp.transpose(jnp.sum(scores, axis=-1), (0, 2, 1))
    numer_local = jnp.einsum(
        "bhij,bjhd->bihd", scores.astype(jnp.bfloat16), values, preferred_element_type=jnp.float32
    )
    numer_local, denom_local = (numer_local, denom_local)
    numer_carried = jnp.einsum(
        "bihm,bhmd->bihd",
        phi_query,
        kv_prefix.astype(jnp.bfloat16),
        preferred_element_type=jnp.float32,
    )
    denom_carried = jnp.einsum(
        "bihm,bhm->bih", phi_query.astype(jnp.float32), key_prefix, precision=lax.Precision.HIGHEST
    )
    numer = numer_local + numer_carried
    denom = denom_local + denom_carried
    output = (numer / denom[..., None]).astype(jnp.bfloat16)
    return output.reshape(batch_size, row_count, head_count * head_dim)


def solution(mesh):
    in_specs = (
        P(None, "seq", "tensor"),
        P(),
        P("seq", "tensor"),
        P("seq", "tensor"),
        P("seq", "tensor"),
        P("tensor", None, None),
    )
    out_specs = P(None, "seq", "tensor")
    fits = mesh.shape["seq"] == 8 and mesh.shape["tensor"] == 4
    return jax.shard_map(
        by_head if fits else on_device, mesh=mesh, in_specs=in_specs, out_specs=out_specs, check_vma=False
    )
```

```python
import functools
import jax
import jax.numpy as jnp
from jax import lax
from jax.experimental import pallas as pl
from jax.experimental.pallas import tpu as pltpu
from jax.sharding import PartitionSpec as P

MESH = pl.DeviceIdType.MESH
F32 = jnp.float32
BF16 = jnp.bfloat16


def head_kernel(
    nz, x_hbm, gain_hbm, wq_ref, wk_ref, wv_ref, dir_hbm, out_ref,
    x_ref, gain_ref, dir_ref, load_sem, pack_sem,
    norm, weight, packed, other, squares, qkv, acc, kv_ref, ksum_ref, made, landed,
    ss_send, ss_recv, b_send, b_recv, z_send, z_recv, x_send, x_recv, c_send, c_recv,
    w_send, w_recv, f_send, f_recv, o_send, o_recv,
):
    s, t = lax.axis_index("seq"), lax.axis_index("tensor")
    z, y = s // 2, s % 2
    ns = 2 * nz
    x, c = t // 2, t % 2
    ty, tx, tc = s + 1 - 2 * y, t + 2 - 4 * x, t + 1 - 2 * c
    tx_c = tx + 1 - 2 * c
    rows, width = x_ref.shape[1], x_ref.shape[2]
    depth = wq_ref.shape[0]
    hd = wq_ref.shape[1] // nz
    full = 4 * width

    def copy(src, dst, send, recv, ds, dt):
        return pltpu.make_async_remote_copy(
            src_ref=src, dst_ref=dst, send_sem=send, recv_sem=recv,
            device_id=(ds, dt), device_id_type=MESH,
        )

    def block(ti, sp):
        return norm.at[ti, pl.ds(pl.multiple_of(sp * rows, rows), rows), :]

    def wrows(sp):
        return weight.at[pl.ds(pl.multiple_of(sp * depth, depth), depth), :]

    loads = [
        pltpu.make_async_copy(x_hbm, x_ref, load_sem.at[0]),
        pltpu.make_async_copy(gain_hbm, gain_ref, load_sem.at[1]),
        pltpu.make_async_copy(dir_hbm.at[z], dir_ref, load_sem.at[2]),
    ]
    loads[0].start()
    for h in range(nz):
        for j, w_ref in enumerate((wq_ref, wk_ref, wv_ref)):
            pltpu.make_async_copy(
                w_ref.at[:, h * hd:(h + 1) * hd],
                packed.at[h, :, j * hd:(j + 1) * hd],
                pack_sem.at[h],
            ).start()
    loads[1].start()
    loads[2].start()

    barrier = pltpu.get_barrier_semaphore()
    for d in range(1, ns):
        pl.semaphore_signal(barrier, inc=1, device_id=((s + d) % ns, t), device_id_type=MESH)
    for d in range(1, 4):
        pl.semaphore_signal(barrier, inc=1, device_id=(s, (t + d) % 4), device_id_type=MESH)

    loads[0].wait()
    for b in range(2):
        wide = x_ref[b].astype(F32)
        part = jnp.sum(wide * wide, axis=-1, keepdims=True)
        lanes = jnp.broadcast_to(part, (rows, 128)).T
        squares[t, :, pl.ds(b * rows, rows)] = lanes[0:8]
    pl.semaphore_wait(barrier, ns - 1 + 3)

    def ss_copy(d):
        return copy(squares.at[t], squares.at[t], ss_send.at[d], ss_recv.at[d], s, (t + d) % 4)

    for d in range(1, 4):
        ss_copy(d).start()

    for h in range(nz):
        pltpu.make_async_copy(packed.at[h], packed.at[h], pack_sem.at[h]).wait()

    def w_copy(to):
        return copy(packed.at[to], wrows(s), w_send.at[to], w_recv.at[z], 2 * to + y, t)

    def each_side(distance, act):
        @pl.when(z - distance >= 0)
        def _():
            act(z - distance)

        @pl.when(z + distance < nz)
        def _():
            act(z + distance)

    def f_copy(zs):
        return copy(wrows(2 * zs + y), wrows(2 * zs + y), f_send.at[zs], f_recv.at[zs], ty, t)

    weight[pl.ds(pl.multiple_of(s * depth, depth), depth), :] = packed[z]
    f_copy(z).start()
    def w_out(distance):
        each_side(distance, lambda to: w_copy(to).start())

    def w_take(distance):
        def act(zs):
            rows_in = wrows(2 * zs + y)
            copy(rows_in, rows_in, w_send.at[zs], w_recv.at[zs], s, t).wait_recv()
            f_copy(zs).start()

        each_side(distance, act)

    for d in range(1, nz):
        w_out(d)

    for d in range(1, 4):
        src = (t + 4 - d) % 4
        copy(squares.at[t], squares.at[src], ss_send.at[d], ss_recv.at[d], s, t).wait_recv()
    total = squares[0] + squares[1] + squares[2] + squares[3]
    loads[1].wait()
    gain = gain_ref[:, pl.ds(pl.multiple_of(t * width, width), width)]

    def normed(b):
        sums = total[0:1, b * rows:(b + 1) * rows]
        column = jnp.broadcast_to(sums, (128, rows)).T
        inv = lax.rsqrt(column[:, 0:1] * (1.0 / full) + 1e-05)
        return (x_ref[b].astype(F32) * inv * gain).astype(BF16)

    for b in range(2):
        @pl.when(y == b)
        def _():
            norm[t, pl.ds(pl.multiple_of(s * rows, rows), rows), :] = normed(b)
            other[...] = normed(1 - b)

    b_copy = copy(other, block(t, s), b_send, b_recv, ty, t)
    b_copy.start()

    def right(sp):
        return copy(block(t, sp), block(t, sp), z_send.at[0, sp], z_recv.at[sp], s + 2, t)

    def left(sp):
        return copy(block(t, sp), block(t, sp), z_send.at[1, sp], z_recv.at[sp], s - 2, t)

    def x_copy(sp):
        return copy(block(t, sp), block(t, sp), x_send.at[sp], x_recv.at[sp], s, tx)

    def c_copy(kind, ti, sp):
        return copy(block(ti, sp), block(ti, sp), c_send.at[kind, sp], c_recv.at[kind, sp], s, tc)

    def spread(sp):
        x_copy(sp).start()
        c_copy(0, t, sp).start()

    def relay(sp):
        copy(block(t, sp), block(tx, sp), x_send.at[sp], x_recv.at[sp], s, tx).wait_recv()
        c_copy(1, tx, sp).start()

    def go(sp):
        @pl.when(z + 1 < nz)
        def _():
            right(sp).start()

        @pl.when(z > 0)
        def _():
            left(sp).start()

    go(s)
    spread(s)
    copy(other, block(t, ty), b_send, b_recv, ty, t).wait_recv()
    go(ty)
    spread(ty)

    def arrivals(k, act):
        for h in range(2):
            from_left = 2 * (z - 1 - k) + (y + h) % 2
            from_right = 2 * (z + 1 + k) + (y + h) % 2

            @pl.when(z - 1 - k >= 0)
            def _():
                act(from_left, 0)

            @pl.when(z + 1 + k < nz)
            def _():
                act(from_right, 1)

    def take(sp, side):
        copy(block(t, sp), block(t, sp), z_send.at[0, sp], z_recv.at[sp], s, t).wait_recv()
        if side == 0:
            @pl.when(z + 1 < nz)
            def _():
                right(sp).start()
        else:
            @pl.when(z > 0)
            def _():
                left(sp).start()
        spread(sp)

    for k in range(nz):
        if k < nz - 1:
            arrivals(k, take)
        if k == 0:
            relay(s)
            relay(ty)
        if k > 0:
            arrivals(k - 1, lambda sp, side: relay(sp))
            w_take(k)

    for sp in range(ns):
        copy(block(t, sp), block(tc, sp), c_send.at[0, sp], c_recv.at[0, sp], s, tc).wait_recv()
        copy(block(tx, sp), block(tx_c, sp), c_send.at[1, sp], c_recv.at[1, sp], s, tc).wait_recv()
    chunk = 2 * rows

    def accumulate(zs, first):
        deep = pl.ds(pl.multiple_of(zs * width, width), width)

        def project(i, carry):
            at = pl.ds(pl.multiple_of(i * chunk, chunk), chunk)
            result = jnp.dot(norm[zs, at, :], weight[deep, :], preferred_element_type=F32)
            acc[at, :] = result if first else acc[at, :] + result
            return carry

        lax.fori_loop(0, nz, project, 0)

    def from_y(zs):
        theirs = wrows(2 * zs + 1 - y)
        copy(theirs, theirs, f_send.at[zs], f_recv.at[zs], ty, t).wait_recv()

    from_y(z)
    accumulate(z, True)
    for d in range(1, nz):
        def add(zs):
            from_y(zs)
            accumulate(zs, False)

        each_side(d, add)
    qkv[...] = acc[...].astype(BF16)

    loads[2].wait()
    directions = dir_ref[...]
    count = directions.shape[0]
    nt = (((1,), (1,)), ((), ()))
    tn = (((0,), (0,)), ((), ()))

    def features(u):
        logits = lax.dot_general(u, directions, nt, preferred_element_type=F32) * hd ** (-0.25)
        wide = u.astype(F32)
        half_sq = 0.5 * jnp.sum(wide * wide, axis=-1, keepdims=True) * hd ** (-0.5)
        return (jnp.exp(logits - half_sq) * count ** (-0.5)).astype(BF16)

    kv_ref[...] = jnp.zeros_like(kv_ref)
    ksum_ref[...] = jnp.zeros_like(ksum_ref)
    row_id = lax.broadcasted_iota(jnp.int32, (rows, rows), 0)
    col_id = lax.broadcasted_iota(jnp.int32, (rows, rows), 1)

    def o_copy(i):
        return copy(made.at[i], landed.at[s], o_send.at[i], o_recv.at[s], i, t)

    def attend(i, carry):
        at = pl.ds(pl.multiple_of(i * rows, rows), rows)
        phi_query = features(qkv[at, 0:hd])
        phi_key = features(qkv[at, hd:2 * hd])
        value = qkv[at, 2 * hd:3 * hd]
        scores = lax.dot_general(phi_query, phi_key, nt, preferred_element_type=F32)
        scores = jnp.where(col_id <= row_id, scores, 0.0)
        ksum = ksum_ref[0:1, :]
        denom = jnp.sum(scores, axis=-1, keepdims=True) + jnp.sum(
            phi_query.astype(F32) * ksum, axis=-1, keepdims=True
        )
        numer = jnp.dot(scores.astype(BF16), value, preferred_element_type=F32) + jnp.dot(
            phi_query, kv_ref[...].astype(BF16), preferred_element_type=F32
        )
        made[i] = (numer / denom).astype(BF16)

        @pl.when(i != s)
        def _():
            o_copy(i).start()

        kv_ref[...] += lax.dot_general(phi_key, value, tn, preferred_element_type=F32)
        ksum_ref[0:1, :] = ksum + jnp.sum(phi_key.astype(F32), axis=0, keepdims=True)
        return carry

    lax.fori_loop(0, ns, attend, 0)

    for sp in range(ns):
        @pl.when(sp != s)
        def _():
            copy(made.at[sp], landed.at[sp], o_send.at[sp], o_recv.at[sp], sp, t).wait_recv()

        @pl.when(sp == s)
        def _():
            landed[sp] = made[sp]

        out_ref[sp % 2, :, (sp // 2) * hd:(sp // 2 + 1) * hd] = landed[sp]

    for d in range(1, 4):
        ss_copy(d).wait_send()
    for d in range(1, nz):
        each_side(d, lambda to: w_copy(to).wait_send())
    for zs in range(nz):
        f_copy(zs).wait_send()
    b_copy.wait_send()
    for sp in range(ns):
        x_copy(sp).wait_send()
        c_copy(0, t, sp).wait_send()
        c_copy(1, tx, sp).wait_send()

        @pl.when((sp // 2 <= z) & (z + 1 < nz))
        def _():
            right(sp).wait_send()

        @pl.when((sp // 2 >= z) & (z > 0))
        def _():
            left(sp).wait_send()

        @pl.when(sp != s)
        def _():
            o_copy(sp).wait_send()


def by_head(inputs, norm_gain, w_query, w_key, w_value, random_head_directions):
    ns = lax.axis_size("seq")
    nz = ns // 2
    batch, rows, width = inputs.shape
    depth, columns = w_query.shape
    hd = columns // nz
    count = random_head_directions.shape[1]
    dma = pltpu.SemaphoreType.DMA
    return pl.pallas_call(
        functools.partial(head_kernel, nz),
        out_shape=jax.ShapeDtypeStruct((batch, rows, columns), BF16),
        in_specs=[pl.BlockSpec(memory_space=pltpu.HBM)] * 6,
        out_specs=pl.BlockSpec(memory_space=pltpu.VMEM),
        scratch_shapes=[
            pltpu.VMEM(inputs.shape, BF16),
            pltpu.VMEM((1, norm_gain.shape[0]), F32),
            pltpu.VMEM((count, hd), BF16),
            pltpu.SemaphoreType.DMA((3,)),
            pltpu.SemaphoreType.DMA((nz,)),
            pltpu.VMEM((4, ns * rows, width), BF16),
            pltpu.VMEM((ns * depth, 3 * hd), BF16),
            pltpu.VMEM((nz, depth, 3 * hd), BF16),
            pltpu.VMEM((rows, width), BF16),
            pltpu.VMEM((4, 8, 2 * rows), F32),
            pltpu.VMEM((ns * rows, 3 * hd), BF16),
            pltpu.VMEM((ns * rows, 3 * hd), F32),
            pltpu.VMEM((count, hd), F32),
            pltpu.VMEM((8, count), F32),
            pltpu.VMEM((ns, rows, hd), BF16),
            pltpu.VMEM((ns, rows, hd), BF16),
            dma((4,)), dma((4,)), dma, dma, dma((2, ns)), dma((ns,)), dma((ns,)), dma((ns,)),
            dma((2, ns)), dma((2, ns)), dma((nz,)), dma((nz,)), dma((nz,)), dma((nz,)),
            dma((ns,)), dma((ns,)),
        ],
        compiler_params=pltpu.CompilerParams(
            collective_id=0, has_side_effects=True, vmem_limit_bytes=48 * 1024 * 1024
        ),
    )(inputs, norm_gain.reshape(1, -1), w_query, w_key, w_value, random_head_directions)


def carried_in(value, axis, join, neutral):
    count, mine = (lax.axis_size(axis), lax.axis_index(axis))
    pieces = jax.tree.map(lambda part: lax.all_gather(part, axis), value)
    total = jax.tree.map(
        lambda part, zero: jnp.full_like(part, 0) + jnp.asarray(zero, part.dtype), value, neutral
    )

    def hop(position, total):
        longer = join(total, jax.tree.map(lambda part: part[position], pieces))
        return jax.tree.map(lambda new, old: jnp.where(position < mine, new, old), longer, total)

    return lax.fori_loop(0, count - 1, hop, total)


def feature_map(direction_product, random_head_directions):
    head_dim = direction_product.shape[-1]
    feature_count = random_head_directions.shape[1]
    attention_logits = jnp.einsum(
        "swcv,clv->swcl",
        direction_product,
        random_head_directions,
        preferred_element_type=jnp.float32,
    ) * head_dim ** (-0.25)
    squared = direction_product.astype(jnp.float32)
    half_sq = 0.5 * jnp.sum(squared * squared, axis=-1, keepdims=True) * head_dim ** (-0.5)
    return (jnp.exp(attention_logits - half_sq) * feature_count ** (-0.5)).astype(jnp.bfloat16)


def add_pair(earlier, later):
    return (earlier[0] + later[0], earlier[1] + later[1])


def on_device(inputs, norm_gain, w_query, w_key, w_value, random_head_directions):
    gathered = lax.all_gather(inputs, "tensor", axis=2, tiled=True)
    batch_size, row_count, full_width = gathered.shape
    wide_in = gathered.astype(jnp.float32)
    inv_rms = lax.rsqrt(jnp.mean(wide_in * wide_in, axis=-1, keepdims=True) + 1e-05)
    normed = (
        (wide_in * inv_rms * norm_gain)
        .astype(jnp.bfloat16)
        .reshape(batch_size * row_count, full_width)
    )

    def add_rows(portion):
        return jnp.dot(normed, portion, preferred_element_type=jnp.float32)

    query_acc = add_rows(lax.all_gather(w_query, "seq", axis=0, tiled=True))
    key_acc = add_rows(lax.all_gather(w_key, "seq", axis=0, tiled=True))
    value_total = add_rows(lax.all_gather(w_value, "seq", axis=0, tiled=True))
    head_count, feature_count, head_dim = random_head_directions.shape

    def split_heads(accum):
        return accum.astype(jnp.bfloat16).reshape(batch_size, row_count, head_count, head_dim)

    query = split_heads(query_acc)
    keys = split_heads(key_acc)
    values = split_heads(value_total)
    phi_query = feature_map(query, random_head_directions)
    phi_key = feature_map(keys, random_head_directions)
    kv_state = jnp.einsum("bjhm,bjhd->bhmd", phi_key, values, preferred_element_type=jnp.float32)
    key_total = jnp.sum(phi_key.astype(jnp.float32), axis=1)
    zero_pair = (jnp.zeros_like(kv_state), jnp.zeros_like(key_total))
    kv_prefix, key_prefix = carried_in((kv_state, key_total), "seq", add_pair, zero_pair)
    lower_triangle_mask = jnp.tril(jnp.ones((row_count, row_count), jnp.bool_))
    scores = jnp.einsum("bihm,bjhm->bhij", phi_query, phi_key, preferred_element_type=jnp.float32)
    scores = jnp.where(lower_triangle_mask, scores, jnp.float32(0.0))
    denom_local = jnp.transpose(jnp.sum(scores, axis=-1), (0, 2, 1))
    numer_local = jnp.einsum(
        "bhij,bjhd->bihd", scores.astype(jnp.bfloat16), values, preferred_element_type=jnp.float32
    )
    numer_local, denom_local = (numer_local, denom_local)
    numer_carried = jnp.einsum(
        "bihm,bhmd->bihd",
        phi_query,
        kv_prefix.astype(jnp.bfloat16),
        preferred_element_type=jnp.float32,
    )
    denom_carried = jnp.einsum(
        "bihm,bhm->bih", phi_query.astype(jnp.float32), key_prefix, precision=lax.Precision.HIGHEST
    )
    numer = numer_local + numer_carried
    denom = denom_local + denom_carried
    output = (numer / denom[..., None]).astype(jnp.bfloat16)
    return output.reshape(batch_size, row_count, head_count * head_dim)


def solution(mesh):
    in_specs = (
        P(None, "seq", "tensor"),
        P(),
        P("seq", "tensor"),
        P("seq", "tensor"),
        P("seq", "tensor"),
        P("tensor", None, None),
    )
    out_specs = P(None, "seq", "tensor")
    fits = mesh.shape["seq"] == 8 and mesh.shape["tensor"] == 4
    return jax.shard_map(
        by_head if fits else on_device, mesh=mesh, in_specs=in_specs, out_specs=out_specs, check_vma=False
    )
```
